256 devices in a mesh: dp: 32 (over z, x_lo, core), grp: 8 (over x_hi, y).
Axes of the slice: x: 4 (x_hi: 2, x_lo: 2; x = x_hi * 2 + x_lo), y: 4, z: 8, core: 2. Of those that a mesh axis runs over, the one named last changes fastest.
Arguments:
- acts: bfloat16 [8, 32768, 1024], P(None, ('dp', 'grp')), may hold values from -24 to 24
- grads: bfloat16 [8, 32768, 1024], P(None, ('dp', 'grp')), may hold values from -0.125 to 0.125
- assign: int32 [8], replicated, may hold values from 0 to 7, each once
- bases_a: bfloat16 [8, 1024, 1024], P('grp', 'dp'), may hold values from -0.1875 to 0.1875
- bases_g: bfloat16 [8, 1024, 1024], P('grp', 'dp'), may hold values from -0.1875 to 0.1875
- eig_a: float32 [8, 1024], P('grp'), may hold values from 0.3 to 2
- eig_g: float32 [8, 1024], P('grp'), may hold values from 0.3 to 2
Outputs:
- factor_a: float32 [8, 1024, 1024], P('grp', 'dp')
- factor_g: float32 [8, 1024, 1024], P('grp', 'dp')
- precond: bfloat16 [8, 1024, 1024], P(None, 'dp')
The draws below stay inside these ranges and needn't reach their ends.
Inputs may be any that keep to these rules, and one draw needn't show every extreme that they name: assign is a permutation of the slots; slot k belongs to the owner group k // (8 / number of groups).
All inputs are finite; a program needn't handle non-finite values.
Results may differ from the reference program's by a relative error of at most 0.0085.
Values may be sent and summed in bfloat16 or wider, within the bound.
No kernel may reach another device: no remote copies, remote signals or barrier semaphores. Data moves between devices by JAX's collectives and lax.ppermute only.
A program may use at most 128 MiB of HBM per device.

```python
import math
import jax
import jax.numpy as jnp
from jax import lax

D = 1024
PROJ = 8
TOKENS = 32768


def with_spikes(values, own_key, source, target, parts, factor):
    owner, partner = [(jnp.arange(values.shape[dim]) // (values.shape[dim] // parts)).reshape([-1 if axis == dim else 1 for axis in range(values.ndim)]) for dim in (source, target)]
    chosen = jax.random.permutation(own_key, parts)[partner]
    strong = (owner == chosen) | (owner == (partner + parts // 2) % parts)
    return jnp.where(strong, factor * values, values)


def steps_of(stream_key, shape, cuts, least, top_value):
    factor_of, own = 1.0, jax.random.fold_in(stream_key, 6)
    for position, blocks in cuts:
        draws = jnp.exp(jax.random.uniform(jax.random.fold_in(own, position), (blocks,), jnp.float32, least / len(cuts), top_value / len(cuts)))
        factor_of = factor_of * jnp.repeat(draws, shape[position] // blocks).reshape([-1 if axis == position else 1 for axis in range(len(shape))])
    return factor_of


def centred(stream_key, dims, width, most, split=(), held_as=jnp.bfloat16):
    entries = jax.random.normal(stream_key, dims, jnp.float32) * width
    if len(split) > 0:
        entries = steps_of(stream_key, dims, split, -0.22, 0.18) * entries
    return jnp.clip(entries, min=-most, max=most).astype(held_as)


def gaussian_with(own_key, extent, scale, reach, split, heavy, kind=jnp.bfloat16):
    array = scale * jax.random.normal(own_key, extent, jnp.float32)
    if split:
        array = array * steps_of(own_key, extent, split, -0.22, 0.18)
    return jnp.clip(with_spikes(array, jax.random.fold_in(own_key, 3), *heavy), -reach, reach).astype(kind)


def setup_inputs(seed: int = 0) -> dict:
    keys = jax.random.split(jax.random.key(seed), 8)
    acts = gaussian_with(keys[0], (PROJ, TOKENS, D), 1.0, 24.0, ((1, 256),), (1, 2, 256, 6.0))
    grads = gaussian_with(keys[1], (PROJ, TOKENS, D), (TOKENS ** -0.5), 0.125, ((1, 256),), (1, 2, 256, 6.0))
    assign = jax.random.permutation(keys[2], PROJ).astype(jnp.int32)
    bases_a = centred(keys[3], (PROJ, D, D), D ** -0.5, 0.1875, ((0, 8), (1, 32)))
    bases_g = centred(keys[4], (PROJ, D, D), D ** -0.5, 0.1875, ((0, 8), (1, 32)))
    eig_a = jnp.clip(jnp.exp(math.log(2.0) - 1.89712 * jax.random.uniform(keys[5], (PROJ, D), jnp.float32) ** steps_of(keys[5], (PROJ, D), ((0, 8),), -0.2, 0.2)), 0.3, 2.0)
    eig_g = jnp.clip(jnp.exp(math.log(2.0) - 1.89712 * jax.random.uniform(keys[6], (PROJ, D), jnp.float32) ** steps_of(keys[6], (PROJ, D), ((0, 8),), -0.2, 0.2)), 0.3, 2.0)
    return dict(acts=acts, grads=grads, assign=assign, bases_a=bases_a, bases_g=bases_g, eig_a=eig_a, eig_g=eig_g)


damping_term = 0.1


def reference(acts, grads, assign, bases_a, bases_g, eig_a, eig_g):
    owned_proj = jnp.argsort(assign).astype(jnp.int32)
    list_a = []
    list_g = []
    list_result = []
    for slot in range(PROJ):
        act_rows = acts[owned_proj[slot]]
        grad_rows = grads[owned_proj[slot]]
        gram_a = jnp.dot(act_rows.T, act_rows, preferred_element_type=jnp.float32) / TOKENS
        gram_g = jnp.dot(grad_rows.T, grad_rows, preferred_element_type=jnp.float32)
        grad_w = jnp.dot(grad_rows.T, act_rows, preferred_element_type=jnp.float32)
        basis_a = bases_a[slot]
        basis_g = bases_g[slot]
        rotated = jnp.dot(basis_g.astype(jnp.float32).T, grad_w, precision=lax.Precision.HIGHEST, preferred_element_type=jnp.float32).astype(jnp.bfloat16)
        mixed = jnp.dot(rotated, basis_a, preferred_element_type=jnp.float32)
        divisor = eig_g[slot][:, None] * eig_a[slot][None, :] + damping_term
        scaled = (mixed / divisor).astype(jnp.bfloat16)
        back = jnp.dot(scaled, basis_a.T, preferred_element_type=jnp.float32).astype(jnp.bfloat16)
        result = jnp.dot(basis_g, back, preferred_element_type=jnp.float32).astype(jnp.bfloat16)
        list_a.append(gram_a)
        list_g.append(gram_g)
        list_result.append(result)
    owner_result = jnp.stack(list_result)
    precond = jnp.take(owner_result, assign.astype(jnp.int32), axis=0)
    return jnp.stack(list_a), jnp.stack(list_g), precond
```

```python
import jax
import jax.numpy as jnp
from jax import lax
from jax.experimental import pallas as pl
from jax.experimental.pallas import tpu as pltpu
from jax.sharding import Mesh, PartitionSpec as P

damping_term = 0.1
bf16, f32 = jnp.bfloat16, jnp.float32
GRP = ("xh", "y")
DP = ("z", "xl", "core")
CHIPS = ("z", "xl")
contract_first = (((0,), (0,)), ((), ()))
contract_last = (((1,), (1,)), ((), ()))


def pick_kernel(owned, src, dst):
    dst[...] = src[...]


def pick(owned, x):
    n, rows, width = x.shape
    return pl.pallas_call(
        pick_kernel,
        grid_spec=pltpu.PrefetchScalarGridSpec(
            num_scalar_prefetch=1,
            grid=(n,),
            in_specs=[pl.BlockSpec((1, rows, width), lambda i, owned: (owned[i], 0, 0))],
            out_specs=pl.BlockSpec((1, rows, width), lambda i, owned: (i, 0, 0)),
        ),
        out_shape=jax.ShapeDtypeStruct(x.shape, x.dtype),
    )(owned, x)


def body(acts, grads, assign, bases_a, bases_g, eig_a, eig_g):
    n_proj = acts.shape[0]
    width = acts.shape[2]
    n_z, n_xl, n_core = (lax.axis_size(a) for a in DP)
    n_grp = lax.axis_size("xh") * lax.axis_size("y")
    n_dp = n_z * n_xl * n_core
    rows = width // n_dp
    tokens = acts.shape[1] * n_dp * n_grp
    z, xl, core = (lax.axis_index(a) for a in DP)

    bases = lax.all_gather(jnp.stack([bases_g[0], bases_a[0]]), DP, axis=1, tiled=True)
    full_g, full_a = bases[0], bases[1]

    slot_ids = lax.broadcasted_iota(jnp.int32, (n_proj, n_proj), 0)
    proj_ids = lax.broadcasted_iota(jnp.int32, (n_proj, n_proj), 1)
    owned = jnp.sum(jnp.where(assign[None, :] == slot_ids, proj_ids, 0), axis=1)
    own_g = lax.all_to_all(pick(owned, grads), GRP, 0, 0, tiled=True).reshape(-1, width)
    own_a = lax.all_to_all(pick(owned, acts), GRP, 0, 0, tiled=True).reshape(-1, width)

    def dot_first(x, y):
        return lax.dot_general(x, y, contract_first, preferred_element_type=f32)

    def swap(x, axis):
        return lax.ppermute(x, axis, [(0, 1), (1, 0)])

    def core_half(total, wire):
        parts = total.reshape(n_z * n_xl, n_core, rows, width)
        keep = lax.dynamic_index_in_dim(parts, core, 1, False)
        give = lax.dynamic_index_in_dim(parts, 1 - core, 1, False)
        return keep + swap(give.astype(wire), "core").astype(f32)

    half_g = core_half(dot_first(own_g, own_g), f32)
    half_a = core_half(dot_first(own_a, own_a) / tokens, f32)
    factors = lax.psum_scatter(
        jnp.concatenate([half_a, half_g], axis=1).reshape(-1, width),
        CHIPS,
        scatter_dimension=0,
        tiled=True,
    )
    factor_a, factor_g = factors[:rows], factors[rows:]

    turned = jnp.dot(own_g, full_g, preferred_element_type=f32).astype(bf16)
    part = dot_first(turned, own_a).reshape(n_xl, n_core, n_z, rows, width)
    keep = lax.dynamic_index_in_dim(part, core, 1, False)
    give = lax.dynamic_index_in_dim(part, 1 - core, 1, False).astype(bf16)
    pair = (keep + swap(give, "core").astype(f32)).astype(bf16)
    pair = jnp.transpose(pair, (1, 0, 2, 3)).reshape(n_z * n_xl, rows, width)
    rotated = jnp.sum(
        lax.all_to_all(pair, CHIPS, 0, 0, tiled=True).astype(f32), axis=0
    ).astype(bf16)
    spread = jnp.broadcast_to(rotated[None], (n_z, rows, width))
    rotated = lax.all_to_all(spread, "z", 0, 0, tiled=True).reshape(n_z * rows, width)

    quarter = n_z * rows
    first = (xl * n_core + core) * quarter
    eig_rows = lax.dynamic_slice_in_dim(eig_g[0], first, quarter, 0)
    divisor = eig_rows[:, None] * eig_a[0][None, :] + damping_term
    mixed = jnp.dot(rotated, full_a, preferred_element_type=f32)
    scaled = (mixed / divisor).astype(bf16)
    back = lax.dot_general(scaled, full_a, contract_last, preferred_element_type=f32).astype(bf16)
    family = n_xl * n_core * rows
    left = lax.dynamic_slice(full_g, (z * family, first), (family, quarter))
    result = jnp.dot(left, back, preferred_element_type=f32)

    def fold(x, axis, index):
        halves = x.reshape(2, -1, width)
        keep = lax.dynamic_index_in_dim(halves, index, 0, False)
        give = lax.dynamic_index_in_dim(halves, 1 - index, 0, False)
        return keep + swap(give, axis)

    result = fold(fold(result, "xl", xl), "core", core).astype(bf16)
    spread = jnp.broadcast_to(result[None], (n_grp, rows, width))
    gathered = lax.all_to_all(spread, GRP, 0, 0, tiled=True)
    precond = jnp.take(gathered, assign, axis=0)
    return (factor_a[None], factor_g[None], precond)


def solution(mesh):
    cut = Mesh(mesh.devices.reshape(8, 2, 2, 2, 4), DP + GRP)
    in_specs = (
        P(None, DP + GRP, None),
        P(None, DP + GRP, None),
        P(),
        P(GRP, DP, None),
        P(GRP, DP, None),
        P(GRP, None),
        P(GRP, None),
    )
    out_specs = (P(GRP, DP, None), P(GRP, DP, None), P(None, DP, None))
    return jax.shard_map(body, mesh=cut, in_specs=in_specs, out_specs=out_specs, check_vma=False)
```

```python
import jax
import jax.numpy as jnp
from jax import lax
from jax.experimental import pallas as pl
from jax.experimental.pallas import tpu as pltpu
from jax.sharding import Mesh, PartitionSpec as P

damping_term = 0.1
bf16, f32 = jnp.bfloat16, jnp.float32
GRP = ("xh", "y")
DP = ("z", "xl", "core")
contract_first = (((0,), (0,)), ((), ()))
contract_last = (((1,), (1,)), ((), ()))


def pick_kernel(assign, grads, acts, dst, buf, got, put):
    n = grads.shape[0]
    loads, stores = [], []
    for slot in range(n):
        owned = jnp.int32(0)
        for p in range(n):
            owned = owned + jnp.where(assign[p] == slot, p, 0)
        for i, src in enumerate((grads, acts)):
            loads.append(pltpu.make_async_copy(src.at[owned], buf.at[slot, i], got.at[slot, i]))
            stores.append(pltpu.make_async_copy(buf.at[slot, i], dst.at[slot, i], put.at[slot, i]))
    for load in loads:
        load.start()
    for load, store in zip(loads, stores):
        load.wait()
        store.start()
    for store in stores:
        store.wait()


def pick(assign, grads, acts):
    n, rows, width = grads.shape
    both = (n, 2, rows, width)
    return pl.pallas_call(
        pick_kernel,
        in_specs=[pl.BlockSpec(memory_space=pltpu.SMEM)] + [pl.BlockSpec(memory_space=pl.ANY)] * 2,
        out_specs=pl.BlockSpec(memory_space=pl.ANY),
        out_shape=jax.ShapeDtypeStruct(both, grads.dtype),
        scratch_shapes=[
            pltpu.VMEM(both, grads.dtype),
            pltpu.SemaphoreType.DMA((n, 2)),
            pltpu.SemaphoreType.DMA((n, 2)),
        ],
        cost_estimate=pl.CostEstimate(flops=0, bytes_accessed=8 * grads.size, transcendentals=0),
    )(assign, grads, acts)


def body(acts, grads, assign, bases_a, bases_g, eig_a, eig_g):
    n_proj = acts.shape[0]
    width = acts.shape[2]
    n_z, n_xl, n_core = (lax.axis_size(a) for a in DP)
    n_grp = lax.axis_size("xh") * lax.axis_size("y")
    n_dp = n_z * n_xl * n_core
    rows = width // n_dp
    tokens = acts.shape[1] * n_dp * n_grp
    z, xl, core = (lax.axis_index(a) for a in DP)

    def swap(x, axis):
        return lax.ppermute(x, axis, [(0, 1), (1, 0)])

    def in_order(index, mine, other):
        return jnp.where(index == 0, mine, other), jnp.where(index == 0, other, mine)

    mine, give = in_order(core, bases_g[0], bases_a[0])
    some = jnp.concatenate(in_order(core, mine, swap(give, "core")))
    other, send = lax.optimization_barrier((swap(some, "xl"), pick(assign, grads, acts)))
    some = jnp.concatenate(in_order(xl, some, other))
    some = lax.all_gather(some, "z", axis=0, tiled=True)
    full_g, full_a = in_order(core, some, swap(some, "core"))

    own = lax.all_to_all(send, GRP, 0, 0, tiled=True)
    own, full_g, full_a = lax.optimization_barrier((own, full_g, full_a))
    own_g = own[:, 0].reshape(-1, width)
    own_a = own[:, 1].reshape(-1, width)

    def dot_first(x, y):
        return lax.dot_general(x, y, contract_first, preferred_element_type=f32)

    def core_sum(total):
        parts = total.reshape(n_z, n_xl, n_core, rows, width)
        keep = lax.dynamic_index_in_dim(parts, core, 2, False)
        give = lax.dynamic_index_in_dim(parts, 1 - core, 2, False)
        return (keep + swap(give.astype(bf16), "core").astype(f32)).astype(bf16)

    def owner_rows(mine):
        keep = lax.dynamic_index_in_dim(mine, xl, 0, False)
        give = lax.dynamic_index_in_dim(mine, 1 - xl, 0, False)
        return keep.astype(f32) + swap(give, "xl").astype(f32)

    turned = jnp.dot(own_g, full_g, preferred_element_type=f32).astype(bf16)
    half = width // n_core
    give = lax.dynamic_slice_in_dim(turned, (1 - core) * half, half, 1)
    keep = lax.dynamic_slice_in_dim(turned, core * half, half, 1)
    give = swap(dot_first(give, own_a).astype(bf16), "core")
    kept = lax.optimization_barrier(dot_first(keep, own_a))
    pair = (kept + give.astype(f32)).astype(bf16)
    pair = pair.reshape(n_xl * n_z, rows, width)
    own_g, own_a, pair = lax.optimization_barrier((own_g, own_a, pair))
    half_g = core_sum(dot_first(own_g, own_g))
    half_a = core_sum(dot_first(own_a, own_a) / tokens)
    rotated = jnp.sum(
        lax.all_to_all(pair, ("xl", "z"), 0, 0, tiled=True).astype(f32), axis=0
    ).astype(bf16)
    rotated, half_g, half_a = lax.optimization_barrier((rotated, half_g, half_a))
    halves = jnp.concatenate([half_g, half_a], axis=1).reshape(-1, width)
    sums = lax.psum_scatter(halves, "z", scatter_dimension=0, tiled=True)
    sums = sums.reshape(2, n_xl, rows, width)
    factor_g, factor_a = owner_rows(sums[0]), owner_rows(sums[1])
    spread = jnp.broadcast_to(rotated[None], (n_z, rows, width))
    rotated = lax.all_to_all(spread, "z", 0, 0, tiled=True).reshape(n_z * rows, width)

    quarter = n_z * rows
    first = (core * n_xl + xl) * quarter
    eig_rows = lax.dynamic_slice_in_dim(eig_g[0], first, quarter, 0)
    divisor = eig_rows[:, None] * eig_a[0][None, :] + damping_term
    mixed = jnp.dot(rotated, full_a, preferred_element_type=f32)
    scaled = (mixed / divisor).astype(bf16)
    back = lax.dot_general(scaled, full_a, contract_last, preferred_element_type=f32).astype(bf16)
    family = n_xl * n_core * rows
    left = lax.dynamic_slice(full_g, (z * family, first), (family, quarter))
    result = jnp.dot(left, back, preferred_element_type=f32)

    def fold(x, axis, index):
        halves = x.reshape(2, -1, width)
        keep = lax.dynamic_index_in_dim(halves, index, 0, False)
        give = lax.dynamic_index_in_dim(halves, 1 - index, 0, False)
        return keep + swap(give, axis)

    result = fold(fold(result, "xl", xl), "core", core).astype(bf16)
    spread = jnp.broadcast_to(result[None], (n_grp, rows, width))
    gathered = lax.all_to_all(spread, GRP, 0, 0, tiled=True)
    gathered, factor_a, factor_g = lax.optimization_barrier((gathered, factor_a, factor_g))
    precond = jnp.take(gathered, assign, axis=0, mode="clip")
    return (factor_a[None], factor_g[None], precond)


def solution(mesh):
    cut = Mesh(mesh.devices.reshape(8, 2, 2, 2, 4), DP + GRP)
    in_specs = (
        P(None, DP + GRP, None),
        P(None, DP + GRP, None),
        P(),
        P(GRP, DP, None),
        P(GRP, DP, None),
        P(GRP, None),
        P(GRP, None),
    )
    out_specs = (P(GRP, DP, None), P(GRP, DP, None), P(None, DP, None))
    return jax.shard_map(body, mesh=cut, in_specs=in_specs, out_specs=out_specs, check_vma=False)
```

```python
import jax
import jax.numpy as jnp
from jax import lax
from jax.experimental import pallas as pl
from jax.experimental.pallas import tpu as pltpu
from jax.sharding import Mesh, PartitionSpec as P

damping_term = 0.1
bf16, f32 = jnp.bfloat16, jnp.float32
GRP = ("xh", "y")
DP = ("z", "xl", "core")
contract_first = (((0,), (0,)), ((), ()))
contract_last = (((1,), (1,)), ((), ()))


def pick_kernel(assign, grads, acts, dst, buf, got, put):
    n = grads.shape[0]
    loads, stores = [], []
    for slot in range(n):
        owned = jnp.int32(0)
        for p in range(n):
            owned = owned + jnp.where(assign[p] == slot, p, 0)
        for i, src in enumerate((grads, acts)):
            loads.append(pltpu.make_async_copy(src.at[owned], buf.at[slot, i], got.at[slot, i]))
            stores.append(pltpu.make_async_copy(buf.at[slot, i], dst.at[slot, i], put.at[slot, i]))
    for load in loads:
        load.start()
    for load, store in zip(loads, stores):
        load.wait()
        store.start()
    for store in stores:
        store.wait()


def pick(assign, grads, acts):
    n, rows, width = grads.shape
    both = (n, 2, rows, width)
    return pl.pallas_call(
        pick_kernel,
        in_specs=[pl.BlockSpec(memory_space=pltpu.SMEM)] + [pl.BlockSpec(memory_space=pl.ANY)] * 2,
        out_specs=pl.BlockSpec(memory_space=pl.ANY),
        out_shape=jax.ShapeDtypeStruct(both, grads.dtype),
        scratch_shapes=[
            pltpu.VMEM(both, grads.dtype),
            pltpu.SemaphoreType.DMA((n, 2)),
            pltpu.SemaphoreType.DMA((n, 2)),
        ],
        cost_estimate=pl.CostEstimate(flops=0, bytes_accessed=8 * grads.size, transcendentals=0),
    )(assign, grads, acts)


def weave_kernel(where, mine, other, out_g, out_a, buf, got, put):
    loads = [pltpu.make_async_copy(x, buf.at[i], got.at[i]) for i, x in enumerate((mine, other))]
    for load in loads:
        load.start()
    for load in loads:
        load.wait()
    stores = []
    for b, out in enumerate((out_g, out_a)):
        for c in range(2):
            held = lax.rem(where[0] + c, 2)
            stores.append(
                pltpu.make_async_copy(buf.at[held, :, b], out.at[:, :, c], put.at[2 * b + c])
            )
    for store in stores:
        store.start()
    for store in stores:
        store.wait()


def weave(core, mine, other):
    n_z, _, n_xl, rows, width = mine.shape
    whole = jax.ShapeDtypeStruct((n_z, n_xl, 2, rows, width), mine.dtype)
    return pl.pallas_call(
        weave_kernel,
        in_specs=[pl.BlockSpec(memory_space=pltpu.SMEM)] + [pl.BlockSpec(memory_space=pl.ANY)] * 2,
        out_specs=[pl.BlockSpec(memory_space=pl.ANY)] * 2,
        out_shape=[whole, whole],
        scratch_shapes=[
            pltpu.VMEM((2,) + mine.shape, mine.dtype),
            pltpu.SemaphoreType.DMA((2,)),
            pltpu.SemaphoreType.DMA((4,)),
        ],
        compiler_params=pltpu.CompilerParams(vmem_limit_bytes=32 << 20),
    )(core.reshape(1), mine, other)


def spread_sum_kernel(src, out):
    total = src[0].astype(jnp.float32)
    for i in range(1, src.shape[0]):
        total = total + src[i].astype(jnp.float32)
    total = total.astype(out.dtype)
    for i in range(out.shape[0]):
        out[i] = total


def spread_sum(parts, copies):
    return pl.pallas_call(
        spread_sum_kernel,
        in_specs=[pl.BlockSpec(memory_space=pltpu.VMEM)],
        out_specs=pl.BlockSpec(memory_space=pltpu.VMEM),
        out_shape=jax.ShapeDtypeStruct((copies,) + parts.shape[1:], parts.dtype),
        compiler_params=pltpu.CompilerParams(vmem_limit_bytes=16 << 20),
    )(parts)


def chain_kernel(rotated, basis, left, eig_rows, eig_cols, out):
    mixed = jnp.dot(rotated[...], basis[...], preferred_element_type=f32)
    scaled = (mixed / (eig_rows[...] * eig_cols[...] + damping_term)).astype(bf16)
    back = lax.dot_general(scaled, basis[...], contract_last, preferred_element_type=f32)
    out[...] = jnp.dot(left[...], back.astype(bf16), preferred_element_type=f32)


def chain(rotated, basis, left, eig_rows, eig_cols):
    return pl.pallas_call(
        chain_kernel,
        in_specs=[pl.BlockSpec(memory_space=pltpu.VMEM)] * 5,
        out_specs=pl.BlockSpec(memory_space=pltpu.VMEM),
        out_shape=jax.ShapeDtypeStruct((left.shape[0], basis.shape[0]), f32),
        compiler_params=pltpu.CompilerParams(vmem_limit_bytes=32 << 20),
    )(rotated, basis, left, eig_rows, eig_cols)


def body(acts, grads, assign, bases_a, bases_g, eig_a, eig_g):
    n_proj = acts.shape[0]
    width = acts.shape[2]
    n_z, n_xl, n_core = (lax.axis_size(a) for a in DP)
    n_grp = lax.axis_size("xh") * lax.axis_size("y")
    n_dp = n_z * n_xl * n_core
    rows = width // n_dp
    tokens = acts.shape[1] * n_dp * n_grp
    z, xl, core = (lax.axis_index(a) for a in DP)

    def swap(x, axis):
        return lax.ppermute(x, axis, [(0, 1), (1, 0)])

    def in_order(index, mine, other):
        return jnp.where(index == 0, mine, other), jnp.where(index == 0, other, mine)

    mine = jnp.stack([bases_g[0], bases_a[0]])
    other, send = lax.optimization_barrier((swap(mine, "xl"), pick(assign, grads, acts)))
    mine = jnp.stack(in_order(xl, mine, other), axis=1).reshape(-1, width)
    mine = lax.all_gather(mine, "z", axis=0, tiled=False)
    mine = mine.reshape(n_z, 2, n_xl, rows, width)
    full_g, full_a = (x.reshape(width, width) for x in weave(core, mine, swap(mine, "core")))

    own = lax.all_to_all(send, GRP, 0, 0, tiled=True)
    own, full_g, full_a = lax.optimization_barrier((own, full_g, full_a))
    own_g = own[:, 0].reshape(-1, width)
    own_a = own[:, 1].reshape(-1, width)

    def dot_first(x, y):
        return lax.dot_general(x, y, contract_first, preferred_element_type=f32)

    def core_sum(total):
        parts = total.reshape(n_z, n_xl, n_core, rows, width)
        keep = lax.dynamic_index_in_dim(parts, core, 2, False)
        give = lax.dynamic_index_in_dim(parts, 1 - core, 2, False)
        return (keep + swap(give.astype(bf16), "core").astype(f32)).astype(bf16)

    def owner_rows(mine):
        keep = lax.dynamic_index_in_dim(mine, xl, 0, False)
        give = lax.dynamic_index_in_dim(mine, 1 - xl, 0, False)
        return keep.astype(f32) + swap(give, "xl").astype(f32)

    turned = jnp.dot(own_g, full_g, preferred_element_type=f32).astype(bf16)
    half = width // n_core
    give = lax.dynamic_slice_in_dim(turned, (1 - core) * half, half, 1)
    keep = lax.dynamic_slice_in_dim(turned, core * half, half, 1)
    give = swap(dot_first(give, own_a).astype(bf16), "core")
    kept = lax.optimization_barrier(dot_first(keep, own_a).astype(bf16))
    pair = (kept.astype(f32) + give.astype(f32)).astype(bf16)
    pair = pair.reshape(n_xl * n_z, rows, width)
    own_g, own_a, pair = lax.optimization_barrier((own_g, own_a, pair))
    half_g = core_sum(dot_first(own_g, own_g))
    half_a = core_sum(dot_first(own_a, own_a) / tokens)
    spread = spread_sum(lax.all_to_all(pair, ("xl", "z"), 0, 0, tiled=True), n_z)
    halves = jnp.concatenate([half_g, half_a], axis=1).reshape(-1, width)
    spread, halves = lax.optimization_barrier((spread, halves))
    sums = lax.psum_scatter(halves, "z", scatter_dimension=0, tiled=True)
    sums = sums.reshape(2, n_xl, rows, width)
    factor_g, factor_a = owner_rows(sums[0]), owner_rows(sums[1])
    rotated = lax.all_to_all(spread, "z", 0, 0, tiled=True).reshape(n_z * rows, width)

    quarter = n_z * rows
    first = (core * n_xl + xl) * quarter
    eig_rows = lax.dynamic_slice_in_dim(eig_g[0], first, quarter, 0)
    family = n_xl * n_core * rows
    left = lax.dynamic_slice(full_g, (z * family, first), (family, quarter))
    result = chain(rotated, full_a, left, eig_rows[:, None], eig_a)

    def fold(x, axis, index):
        halves = x.reshape(2, -1, width)
        keep = lax.dynamic_index_in_dim(halves, index, 0, False)
        give = lax.dynamic_index_in_dim(halves, 1 - index, 0, False)
        return keep + swap(give, axis)

    result = fold(fold(result, "xl", xl), "core", core).astype(bf16)
    spread = jnp.broadcast_to(result[None], (n_grp, rows, width))
    gathered = lax.all_to_all(spread, GRP, 0, 0, tiled=True)
    gathered, factor_a, factor_g = lax.optimization_barrier((gathered, factor_a, factor_g))
    precond = jnp.take(gathered, assign, axis=0, mode="clip")
    return (factor_a[None], factor_g[None], precond)


def solution(mesh):
    cut = Mesh(mesh.devices.reshape(8, 2, 2, 2, 4), DP + GRP)
    in_specs = (
        P(None, DP + GRP, None),
        P(None, DP + GRP, None),
        P(),
        P(GRP, DP, None),
        P(GRP, DP, None),
        P(GRP, None),
        P(GRP, None),
    )
    out_specs = (P(GRP, DP, None), P(GRP, DP, None), P(None, DP, None))
    return jax.shard_map(body, mesh=cut, in_specs=in_specs, out_specs=out_specs, check_vma=False)
```

```python
import jax
import jax.numpy as jnp
from jax import lax
from jax.experimental import pallas as pl
from jax.experimental.pallas import tpu as pltpu
from jax.sharding import Mesh, PartitionSpec as P

damping_term = 0.1
bf16, f32 = jnp.bfloat16, jnp.float32
GRP = ("xh", "y")
DP = ("z", "xl", "core")
contract_first = (((0,), (0,)), ((), ()))
contract_last = (((1,), (1,)), ((), ()))


def pick_kernel(assign, grads, acts, dst, buf, got, put):
    n = grads.shape[0]
    loads, stores = [], []
    for slot in range(n):
        owned = jnp.int32(0)
        for p in range(n):
            owned = owned + jnp.where(assign[p] == slot, p, 0)
        for i, src in enumerate((grads, acts)):
            loads.append(pltpu.make_async_copy(src.at[owned], buf.at[slot, i], got.at[slot, i]))
            stores.append(pltpu.make_async_copy(buf.at[slot, i], dst.at[slot, i], put.at[slot, i]))
    for load in loads:
        load.start()
    for load, store in zip(loads, stores):
        load.wait()
        store.start()
    for store in stores:
        store.wait()


def pick(assign, grads, acts):
    n, rows, width = grads.shape
    both = (n, 2, rows, width)
    return pl.pallas_call(
        pick_kernel,
        in_specs=[pl.BlockSpec(memory_space=pltpu.SMEM)] + [pl.BlockSpec(memory_space=pl.ANY)] * 2,
        out_specs=pl.BlockSpec(memory_space=pl.ANY),
        out_shape=jax.ShapeDtypeStruct(both, grads.dtype),
        scratch_shapes=[
            pltpu.VMEM(both, grads.dtype),
            pltpu.SemaphoreType.DMA((n, 2)),
            pltpu.SemaphoreType.DMA((n, 2)),
        ],
        cost_estimate=pl.CostEstimate(flops=0, bytes_accessed=8 * grads.size, transcendentals=0),
    )(assign, grads, acts)


def order_kernel(index, *refs):
    n = len(refs) - 4
    pieces, (out, buf, got, put) = refs[:n], refs[n:]
    loads = [pltpu.make_async_copy(pieces[s], buf.at[s], got.at[s]) for s in range(n)]
    for load in loads:
        load.start()
    for load in loads:
        load.wait()
    stores = [pltpu.make_async_copy(buf.at[index[j]], out.at[j], put.at[j]) for j in range(n)]
    for store in stores:
        store.start()
    for store in stores:
        store.wait()


def order(index, pieces):
    n = len(pieces)
    shape = (n,) + pieces[0].shape
    return pl.pallas_call(
        order_kernel,
        in_specs=[pl.BlockSpec(memory_space=pltpu.SMEM)] + [pl.BlockSpec(memory_space=pl.ANY)] * n,
        out_specs=pl.BlockSpec(memory_space=pl.ANY),
        out_shape=jax.ShapeDtypeStruct(shape, pieces[0].dtype),
        scratch_shapes=[
            pltpu.VMEM(shape, pieces[0].dtype),
            pltpu.SemaphoreType.DMA((n,)),
            pltpu.SemaphoreType.DMA((n,)),
        ],
    )(index, *pieces)


def weave_kernel(where, mine, other, out_g, out_a, buf, got, put):
    loads = [pltpu.make_async_copy(x, buf.at[i], got.at[i]) for i, x in enumerate((mine, other))]
    for load in loads:
        load.start()
    for load in loads:
        load.wait()
    stores = []
    for b, out in enumerate((out_g, out_a)):
        for c in range(2):
            held = lax.rem(where[0] + c, 2)
            stores.append(
                pltpu.make_async_copy(buf.at[held, :, b], out.at[:, :, c], put.at[2 * b + c])
            )
    for store in stores:
        store.start()
    for store in stores:
        store.wait()


def weave(core, mine, other):
    n_z, _, n_xl, rows, width = mine.shape
    whole = jax.ShapeDtypeStruct((n_z, n_xl, 2, rows, width), mine.dtype)
    return pl.pallas_call(
        weave_kernel,
        in_specs=[pl.BlockSpec(memory_space=pltpu.SMEM)] + [pl.BlockSpec(memory_space=pl.ANY)] * 2,
        out_specs=[pl.BlockSpec(memory_space=pl.ANY)] * 2,
        out_shape=[whole, whole],
        scratch_shapes=[
            pltpu.VMEM((2,) + mine.shape, mine.dtype),
            pltpu.SemaphoreType.DMA((2,)),
            pltpu.SemaphoreType.DMA((4,)),
        ],
        compiler_params=pltpu.CompilerParams(vmem_limit_bytes=32 << 20),
    )(core.reshape(1), mine, other)


def spread_sum_kernel(src, out):
    total = src[0].astype(jnp.float32)
    for i in range(1, src.shape[0]):
        total = total + src[i].astype(jnp.float32)
    total = total.astype(out.dtype)
    for i in range(out.shape[0]):
        out[i] = total


def spread_sum(parts, copies):
    return pl.pallas_call(
        spread_sum_kernel,
        in_specs=[pl.BlockSpec(memory_space=pltpu.VMEM)],
        out_specs=pl.BlockSpec(memory_space=pltpu.VMEM),
        out_shape=jax.ShapeDtypeStruct((copies,) + parts.shape[1:], parts.dtype),
        compiler_params=pltpu.CompilerParams(vmem_limit_bytes=16 << 20),
    )(parts)


def chain_kernel(rotated, basis, left, eig_rows, eig_cols, out):
    mixed = jnp.dot(rotated[...], basis[...], preferred_element_type=f32)
    scaled = (mixed / (eig_rows[...] * eig_cols[...] + damping_term)).astype(bf16)
    back = lax.dot_general(scaled, basis[...], contract_last, preferred_element_type=f32)
    out[...] = jnp.dot(left[...], back.astype(bf16), preferred_element_type=f32)


def chain(rotated, basis, left, eig_rows, eig_cols):
    return pl.pallas_call(
        chain_kernel,
        in_specs=[pl.BlockSpec(memory_space=pltpu.VMEM)] * 5,
        out_specs=pl.BlockSpec(memory_space=pltpu.VMEM),
        out_shape=jax.ShapeDtypeStruct((left.shape[0], basis.shape[0]), f32),
        compiler_params=pltpu.CompilerParams(vmem_limit_bytes=32 << 20),
    )(rotated, basis, left, eig_rows, eig_cols)


def body(acts, grads, assign, bases_a, bases_g, eig_a, eig_g):
    n_proj = acts.shape[0]
    width = acts.shape[2]
    n_z, n_xl, n_core = (lax.axis_size(a) for a in DP)
    n_grp = lax.axis_size("xh") * lax.axis_size("y")
    n_dp = n_z * n_xl * n_core
    rows = width // n_dp
    tokens = acts.shape[1] * n_dp * n_grp
    z, xl, core = (lax.axis_index(a) for a in DP)

    def swap(x, axis):
        return lax.ppermute(x, axis, [(0, 1), (1, 0)])

    def in_order(index, mine, other):
        return jnp.where(index == 0, mine, other), jnp.where(index == 0, other, mine)

    mine = jnp.stack([bases_g[0], bases_a[0]])
    other, send = lax.optimization_barrier((swap(mine, "xl"), pick(assign, grads, acts)))
    mine = jnp.stack(in_order(xl, mine, other), axis=1)
    pieces = [mine] * n_z
    up = down = mine
    for s in range(1, n_z // 2 + 1):
        pieces[s] = up = lax.ppermute(up, "z", [(i, (i + 1) % n_z) for i in range(n_z)])
        if s < n_z // 2:
            pieces[-s] = down = lax.ppermute(down, "z", [(i, (i - 1) % n_z) for i in range(n_z)])
    mine = order(lax.rem(z - jnp.arange(n_z, dtype=jnp.int32) + n_z, n_z), pieces)
    full_g, full_a = (x.reshape(width, width) for x in weave(core, mine, swap(mine, "core")))

    own = lax.all_to_all(send, GRP, 0, 0, tiled=True)
    own, full_g, full_a = lax.optimization_barrier((own, full_g, full_a))
    own_g = own[:, 0].reshape(-1, width)
    own_a = own[:, 1].reshape(-1, width)

    def dot_first(x, y):
        return lax.dot_general(x, y, contract_first, preferred_element_type=f32)

    def half_sum(parts, axis, index, dim):
        keep = lax.dynamic_index_in_dim(parts, index, dim, False)
        give = lax.dynamic_index_in_dim(parts, 1 - index, dim, False)
        return (keep.astype(f32) + swap(give.astype(bf16), axis).astype(f32)).astype(bf16)

    def core_sum(total):
        return half_sum(total.reshape(n_z, n_xl, n_core, rows, width), "core", core, 2)

    turned = jnp.dot(own_g, full_g, preferred_element_type=f32).astype(bf16)
    half = width // n_core
    give = lax.dynamic_slice_in_dim(turned, (1 - core) * half, half, 1)
    keep = lax.dynamic_slice_in_dim(turned, core * half, half, 1)
    give = swap(dot_first(give, own_a).astype(bf16), "core")
    kept = lax.optimization_barrier(dot_first(keep, own_a).astype(bf16))
    pair = (kept.astype(f32) + give.astype(f32)).astype(bf16)
    pair = pair.reshape(n_xl * n_z, rows, width)
    own_g, own_a, pair = lax.optimization_barrier((own_g, own_a, pair))
    half_g = core_sum(dot_first(own_g, own_g))
    half_a = core_sum(dot_first(own_a, own_a) / tokens)
    halves = half_sum(jnp.concatenate([half_g, half_a], axis=2), "xl", xl, 1)
    spread = spread_sum(lax.all_to_all(pair, ("xl", "z"), 0, 0, tiled=True), n_z)
    rotated = lax.all_to_all(spread, "z", 0, 0, tiled=True).reshape(n_z * rows, width)

    quarter = n_z * rows
    first = (core * n_xl + xl) * quarter
    eig_rows = lax.dynamic_slice_in_dim(eig_g[0], first, quarter, 0)
    family = n_xl * n_core * rows
    left = lax.dynamic_slice(full_g, (z * family, first), (family, quarter))
    left = left.reshape(n_xl, n_core, rows, quarter).swapaxes(0, 1).reshape(family, quarter)
    result = chain(rotated, full_a, left, eig_rows[:, None], eig_a)

    def fold(x, axis, index):
        halves = x.reshape(2, -1, width)
        keep = lax.dynamic_index_in_dim(halves, index, 0, False)
        give = lax.dynamic_index_in_dim(halves, 1 - index, 0, False)
        return keep + swap(give, axis)

    result = fold(result, "core", core)
    halves, result = lax.optimization_barrier((halves, result))
    sums = jnp.sum(lax.all_to_all(halves, "z", 0, 0, tiled=True).astype(f32), axis=0)
    factor_g, factor_a = sums[:rows], sums[rows:]
    result = fold(result, "xl", xl).astype(bf16)
    pieces = [result]
    for s in range(1, n_grp):
        pieces.append(lax.ppermute(result, GRP, [(i, (i + s) % n_grp) for i in range(n_grp)]))
    me = lax.axis_index(GRP)
    index = lax.rem(me - assign + n_grp, n_grp)[:, None, None]
    precond = jnp.broadcast_to(pieces[0][None], (n_proj, rows, width))
    for s in range(1, n_grp):
        precond = jnp.where(index == s, pieces[s][None], precond)
    return (factor_a[None], factor_g[None], precond)


def solution(mesh):
    cut = Mesh(mesh.devices.reshape(8, 2, 2, 2, 4), DP + GRP)
    in_specs = (
        P(None, DP + GRP, None),
        P(None, DP + GRP, None),
        P(),
        P(GRP, DP, None),
        P(GRP, DP, None),
        P(GRP, None),
        P(GRP, None),
    )
    out_specs = (P(GRP, DP, None), P(GRP, DP, None), P(None, DP, None))
    return jax.shard_map(body, mesh=cut, in_specs=in_specs, out_specs=out_specs, check_vma=False)
```

```python
import jax
import jax.numpy as jnp
from jax import lax
from jax.experimental import pallas as pl
from jax.experimental.pallas import tpu as pltpu
from jax.sharding import Mesh, PartitionSpec as P

damping_term = 0.1
bf16, f32 = jnp.bfloat16, jnp.float32
GRP = ("xh", "y")
DP = ("z", "xl", "core")
contract_first = (((0,), (0,)), ((), ()))
contract_last = (((1,), (1,)), ((), ()))


def pick_kernel(assign, grads, acts, dst, buf, got, put):
    n = grads.shape[0]
    loads, stores = [], []
    for slot in range(n):
        owned = jnp.int32(0)
        for p in range(n):
            owned = owned + jnp.where(assign[p] == slot, p, 0)
        for i, src in enumerate((grads, acts)):
            loads.append(pltpu.make_async_copy(src.at[owned], buf.at[slot, i], got.at[slot, i]))
            stores.append(pltpu.make_async_copy(buf.at[slot, i], dst.at[slot, i], put.at[slot, i]))
    for load in loads:
        load.start()
    for load, store in zip(loads, stores):
        load.wait()
        store.start()
    for store in stores:
        store.wait()


def pick(assign, grads, acts):
    n, rows, width = grads.shape
    both = (n, 2, rows, width)
    return pl.pallas_call(
        pick_kernel,
        in_specs=[pl.BlockSpec(memory_space=pltpu.SMEM)] + [pl.BlockSpec(memory_space=pl.ANY)] * 2,
        out_specs=pl.BlockSpec(memory_space=pl.ANY),
        out_shape=jax.ShapeDtypeStruct(both, grads.dtype),
        scratch_shapes=[
            pltpu.VMEM(both, grads.dtype),
            pltpu.SemaphoreType.DMA((n, 2)),
            pltpu.SemaphoreType.DMA((n, 2)),
        ],
        cost_estimate=pl.CostEstimate(flops=0, bytes_accessed=8 * grads.size, transcendentals=0),
    )(assign, grads, acts)


def order_kernel(index, *refs):
    n = len(refs) - 4
    pieces, (out, buf, got, put) = refs[:n], refs[n:]
    loads = [pltpu.make_async_copy(pieces[s], buf.at[s], got.at[s]) for s in range(n)]
    for load in loads:
        load.start()
    for load in loads:
        load.wait()
    stores = [pltpu.make_async_copy(buf.at[index[j]], out.at[j], put.at[j]) for j in range(n)]
    for store in stores:
        store.start()
    for store in stores:
        store.wait()


def order(index, pieces):
    n = len(pieces)
    shape = (n,) + pieces[0].shape
    return pl.pallas_call(
        order_kernel,
        in_specs=[pl.BlockSpec(memory_space=pltpu.SMEM)] + [pl.BlockSpec(memory_space=pl.ANY)] * n,
        out_specs=pl.BlockSpec(memory_space=pl.ANY),
        out_shape=jax.ShapeDtypeStruct(shape, pieces[0].dtype),
        scratch_shapes=[
            pltpu.VMEM(shape, pieces[0].dtype),
            pltpu.SemaphoreType.DMA((n,)),
            pltpu.SemaphoreType.DMA((n,)),
        ],
    )(index, *pieces)


def weave_kernel(where, mine, other, out_g, out_a, buf, got, put):
    loads = [pltpu.make_async_copy(x, buf.at[i], got.at[i]) for i, x in enumerate((mine, other))]
    for load in loads:
        load.start()
    for load in loads:
        load.wait()
    stores = []
    for b, out in enumerate((out_g, out_a)):
        for c in range(2):
            held = lax.rem(where[0] + c, 2)
            stores.append(
                pltpu.make_async_copy(buf.at[held, :, b], out.at[:, :, c], put.at[2 * b + c])
            )
    for store in stores:
        store.start()
    for store in stores:
        store.wait()


def weave(core, mine, other):
    n_z, _, n_xl, rows, width = mine.shape
    whole = jax.ShapeDtypeStruct((n_z, n_xl, 2, rows, width), mine.dtype)
    return pl.pallas_call(
        weave_kernel,
        in_specs=[pl.BlockSpec(memory_space=pltpu.SMEM)] + [pl.BlockSpec(memory_space=pl.ANY)] * 2,
        out_specs=[pl.BlockSpec(memory_space=pl.ANY)] * 2,
        out_shape=[whole, whole],
        scratch_shapes=[
            pltpu.VMEM((2,) + mine.shape, mine.dtype),
            pltpu.SemaphoreType.DMA((2,)),
            pltpu.SemaphoreType.DMA((4,)),
        ],
        compiler_params=pltpu.CompilerParams(vmem_limit_bytes=32 << 20),
    )(core.reshape(1), mine, other)


def spread_sum_kernel(src, out):
    total = src[0].astype(jnp.float32)
    for i in range(1, src.shape[0]):
        total = total + src[i].astype(jnp.float32)
    total = total.astype(out.dtype)
    for i in range(out.shape[0]):
        out[i] = total


def spread_sum(parts, copies):
    return pl.pallas_call(
        spread_sum_kernel,
        in_specs=[pl.BlockSpec(memory_space=pltpu.VMEM)],
        out_specs=pl.BlockSpec(memory_space=pltpu.VMEM),
        out_shape=jax.ShapeDtypeStruct((copies,) + parts.shape[1:], parts.dtype),
        compiler_params=pltpu.CompilerParams(vmem_limit_bytes=16 << 20),
    )(parts)


def chain_kernel(rotated, basis, left, eig_rows, eig_cols, out):
    mixed = jnp.dot(rotated[...], basis[...], preferred_element_type=f32)
    scaled = (mixed / (eig_rows[...] * eig_cols[...] + damping_term)).astype(bf16)
    back = lax.dot_general(scaled, basis[...], contract_last, preferred_element_type=f32)
    out[...] = jnp.dot(left[...], back.astype(bf16), preferred_element_type=f32)


def chain(rotated, basis, left, eig_rows, eig_cols):
    return pl.pallas_call(
        chain_kernel,
        in_specs=[pl.BlockSpec(memory_space=pltpu.VMEM)] * 5,
        out_specs=pl.BlockSpec(memory_space=pltpu.VMEM),
        out_shape=jax.ShapeDtypeStruct((left.shape[0], basis.shape[0]), f32),
        compiler_params=pltpu.CompilerParams(vmem_limit_bytes=32 << 20),
    )(rotated, basis, left, eig_rows, eig_cols)


def body(acts, grads, assign, bases_a, bases_g, eig_a, eig_g):
    n_proj = acts.shape[0]
    width = acts.shape[2]
    n_z, n_xl, n_core = (lax.axis_size(a) for a in DP)
    n_grp = lax.axis_size("xh") * lax.axis_size("y")
    n_dp = n_z * n_xl * n_core
    rows = width // n_dp
    tokens = acts.shape[1] * n_dp * n_grp
    z, xl, core = (lax.axis_index(a) for a in DP)

    def swap(x, axis):
        return lax.ppermute(x, axis, [(0, 1), (1, 0)])

    def in_order(index, mine, other):
        return jnp.where(index == 0, mine, other), jnp.where(index == 0, other, mine)

    mine = bases_g[0], bases_a[0]
    other, send = lax.optimization_barrier(
        ([swap(x, "xl") for x in mine], pick(assign, grads, acts))
    )
    mine = jnp.stack([jnp.stack(in_order(xl, *x)) for x in zip(mine, other)])
    pieces = [mine] * n_z
    up = down = mine
    for s in range(1, n_z // 2 + 1):
        pieces[s] = up = lax.ppermute(up, "z", [(i, (i + 1) % n_z) for i in range(n_z)])
        if s < n_z // 2:
            pieces[-s] = down = lax.ppermute(down, "z", [(i, (i - 1) % n_z) for i in range(n_z)])
    mine = order(lax.rem(z - jnp.arange(n_z, dtype=jnp.int32) + n_z, n_z), pieces)
    full_g, full_a = (x.reshape(width, width) for x in weave(core, mine, swap(mine, "core")))

    own = lax.all_to_all(send, GRP, 0, 0, tiled=True)
    own, full_g, full_a = lax.optimization_barrier((own, full_g, full_a))
    own_g = own[:, 0].reshape(-1, width)
    own_a = own[:, 1].reshape(-1, width)

    def dot_first(x, y):
        return lax.dot_general(x, y, contract_first, preferred_element_type=f32)

    def half_sum(parts, axis, index, dim):
        keep = lax.dynamic_index_in_dim(parts, index, dim, False)
        give = lax.dynamic_index_in_dim(parts, 1 - index, dim, False)
        return (keep.astype(f32) + swap(give.astype(bf16), axis).astype(f32)).astype(bf16)

    def core_sum(total):
        return half_sum(total.reshape(n_z, n_xl, n_core, rows, width), "core", core, 2)

    turned = jnp.dot(own_g, full_g, preferred_element_type=f32).astype(bf16)
    half = width // n_core
    give = lax.dynamic_slice_in_dim(turned, (1 - core) * half, half, 1)
    keep = lax.dynamic_slice_in_dim(turned, core * half, half, 1)
    give = swap(dot_first(give, own_a).astype(bf16), "core")
    kept = lax.optimization_barrier(dot_first(keep, own_a).astype(bf16))
    pair = (kept.astype(f32) + give.astype(f32)).astype(bf16)
    pair = pair.reshape(n_xl * n_z, rows, width)
    own_g, own_a, pair = lax.optimization_barrier((own_g, own_a, pair))
    half_g = core_sum(dot_first(own_g, own_g))
    half_a = core_sum(dot_first(own_a, own_a) / tokens)
    halves = jnp.concatenate([half_g, half_a], axis=2)
    keep = lax.optimization_barrier(lax.dynamic_index_in_dim(halves, xl, 1, False))
    give = swap(lax.dynamic_index_in_dim(halves, 1 - xl, 1, False), "xl")
    halves = (keep.astype(f32) + give.astype(f32)).astype(bf16)
    spread = spread_sum(lax.all_to_all(pair, ("xl", "z"), 0, 0, tiled=True), n_z)
    rotated = lax.all_to_all(spread, "z", 0, 0, tiled=True).reshape(n_z * rows, width)

    quarter = n_z * rows
    first = (core * n_xl + xl) * quarter
    eig_rows = lax.dynamic_slice_in_dim(eig_g[0], first, quarter, 0)
    family = n_xl * n_core * rows
    left = lax.dynamic_slice(full_g, (z * family, first), (family, quarter))
    left = left.reshape(n_xl, n_core, rows, quarter).swapaxes(0, 1).reshape(family, quarter)
    result = chain(rotated, full_a, left, eig_rows[:, None], eig_a)

    def fold(x, axis, index):
        halves = x.reshape(2, -1, width)
        keep = lax.dynamic_index_in_dim(halves, index, 0, False)
        give = lax.dynamic_index_in_dim(halves, 1 - index, 0, False)
        return keep + swap(give, axis)

    result = fold(result, "core", core)
    halves, result = lax.optimization_barrier((halves, result))
    sums = jnp.sum(lax.all_to_all(halves, "z", 0, 0, tiled=True).astype(f32), axis=0)
    factor_g, factor_a = sums[:rows], sums[rows:]
    result = fold(result, "xl", xl).astype(bf16)
    n_y = lax.axis_size("y")
    pieces = [result] * n_grp
    hops = sorted(
        range(1, n_grp), key=lambda s: -(2 * (s // n_y) + min(s % n_y, n_y - s % n_y))
    )
    for s in hops:
        dx, dy = s // n_y, s % n_y
        moves = [
            (i, (i // n_y + dx) % (n_grp // n_y) * n_y + (i + dy) % n_y) for i in range(n_grp)
        ]
        pieces[s] = lax.ppermute(result, GRP, moves)
    dx = lax.rem(lax.axis_index("xh") - assign // n_y + n_grp // n_y, n_grp // n_y)
    dy = lax.rem(lax.axis_index("y") - lax.rem(assign, n_y) + n_y, n_y)
    index = (dx * n_y + dy)[:, None, None]
    precond = jnp.broadcast_to(pieces[0][None], (n_proj, rows, width))
    for s in range(1, n_grp):
        precond = jnp.where(index == s, pieces[s][None], precond)
    return (factor_a[None], factor_g[None], precond)


def solution(mesh):
    cut = Mesh(mesh.devices.reshape(8, 2, 2, 2, 4), DP + GRP)
    in_specs = (
        P(None, DP + GRP, None),
        P(None, DP + GRP, None),
        P(),
        P(GRP, DP, None),
        P(GRP, DP, None),
        P(GRP, None),
        P(GRP, None),
    )
    out_specs = (P(GRP, DP, None), P(GRP, DP, None), P(None, DP, None))
    return jax.shard_map(body, mesh=cut, in_specs=in_specs, out_specs=out_specs, check_vma=False)
```

```python
import jax
import jax.numpy as jnp
from jax import lax
from jax.experimental import pallas as pl
from jax.experimental.pallas import tpu as pltpu
from jax.sharding import Mesh, PartitionSpec as P

damping_term = 0.1
bf16, f32 = jnp.bfloat16, jnp.float32
GRP = ("xh", "y")
DP = ("z", "xl", "core")
contract_first = (((0,), (0,)), ((), ()))
contract_last = (((1,), (1,)), ((), ()))


def pick_kernel(assign, grads, acts, dst, buf, got, put):
    n = grads.shape[0]
    loads, stores = [], []
    for slot in range(n):
        owned = jnp.int32(0)
        for p in range(n):
            owned = owned + jnp.where(assign[p] == slot, p, 0)
        for i, src in enumerate((grads, acts)):
            loads.append(pltpu.make_async_copy(src.at[owned], buf.at[slot, i], got.at[slot, i]))
            stores.append(pltpu.make_async_copy(buf.at[slot, i], dst.at[slot, i], put.at[slot, i]))
    for load in loads:
        load.start()
    for load, store in zip(loads, stores):
        load.wait()
        store.start()
    for store in stores:
        store.wait()


def pick(assign, grads, acts):
    n, rows, width = grads.shape
    both = (n, 2, rows, width)
    return pl.pallas_call(
        pick_kernel,
        in_specs=[pl.BlockSpec(memory_space=pltpu.SMEM)] + [pl.BlockSpec(memory_space=pl.ANY)] * 2,
        out_specs=pl.BlockSpec(memory_space=pl.ANY),
        out_shape=jax.ShapeDtypeStruct(both, grads.dtype),
        scratch_shapes=[
            pltpu.VMEM(both, grads.dtype),
            pltpu.SemaphoreType.DMA((n, 2)),
            pltpu.SemaphoreType.DMA((n, 2)),
        ],
        cost_estimate=pl.CostEstimate(flops=0, bytes_accessed=8 * grads.size, transcendentals=0),
    )(assign, grads, acts)


def order_kernel(index, *refs):
    n = len(refs) - 4
    pieces, (out, buf, got, put) = refs[:n], refs[n:]
    loads = [pltpu.make_async_copy(pieces[s], buf.at[s], got.at[s]) for s in range(n)]
    for load in loads:
        load.start()
    for load in loads:
        load.wait()
    stores = [pltpu.make_async_copy(buf.at[index[j]], out.at[j], put.at[j]) for j in range(n)]
    for store in stores:
        store.start()
    for store in stores:
        store.wait()


def order(index, pieces):
    n = len(pieces)
    shape = (n,) + pieces[0].shape
    return pl.pallas_call(
        order_kernel,
        in_specs=[pl.BlockSpec(memory_space=pltpu.SMEM)] + [pl.BlockSpec(memory_space=pl.ANY)] * n,
        out_specs=pl.BlockSpec(memory_space=pl.ANY),
        out_shape=jax.ShapeDtypeStruct(shape, pieces[0].dtype),
        scratch_shapes=[
            pltpu.VMEM(shape, pieces[0].dtype),
            pltpu.SemaphoreType.DMA((n,)),
            pltpu.SemaphoreType.DMA((n,)),
        ],
    )(index, *pieces)


def weave_kernel(where, mine, other, out_g, out_a, buf, got, put):
    loads = [pltpu.make_async_copy(x, buf.at[i], got.at[i]) for i, x in enumerate((mine, other))]
    for load in loads:
        load.start()
    for load in loads:
        load.wait()
    stores = []
    for b, out in enumerate((out_g, out_a)):
        for c in range(2):
            held = lax.rem(where[0] + c, 2)
            stores.append(
                pltpu.make_async_copy(buf.at[held, :, b], out.at[:, :, c], put.at[2 * b + c])
            )
    for store in stores:
        store.start()
    for store in stores:
        store.wait()


def weave(core, mine, other):
    n_z, _, n_xl, rows, width = mine.shape
    whole = jax.ShapeDtypeStruct((n_z, n_xl, 2, rows, width), mine.dtype)
    return pl.pallas_call(
        weave_kernel,
        in_specs=[pl.BlockSpec(memory_space=pltpu.SMEM)] + [pl.BlockSpec(memory_space=pl.ANY)] * 2,
        out_specs=[pl.BlockSpec(memory_space=pl.ANY)] * 2,
        out_shape=[whole, whole],
        scratch_shapes=[
            pltpu.VMEM((2,) + mine.shape, mine.dtype),
            pltpu.SemaphoreType.DMA((2,)),
            pltpu.SemaphoreType.DMA((4,)),
        ],
        compiler_params=pltpu.CompilerParams(vmem_limit_bytes=32 << 20),
    )(core.reshape(1), mine, other)


def spread_sum_kernel(src, out):
    total = src[0].astype(jnp.float32)
    for i in range(1, src.shape[0]):
        total = total + src[i].astype(jnp.float32)
    total = total.astype(out.dtype)
    for i in range(out.shape[0]):
        out[i] = total


def spread_sum(parts, copies):
    return pl.pallas_call(
        spread_sum_kernel,
        in_specs=[pl.BlockSpec(memory_space=pltpu.VMEM)],
        out_specs=pl.BlockSpec(memory_space=pltpu.VMEM),
        out_shape=jax.ShapeDtypeStruct((copies,) + parts.shape[1:], parts.dtype),
        compiler_params=pltpu.CompilerParams(vmem_limit_bytes=16 << 20),
    )(parts)


def chain_kernel(rotated, basis, left, eig_rows, eig_cols, out):
    mixed = jnp.dot(rotated[...], basis[...], preferred_element_type=f32)
    scaled = (mixed / (eig_rows[...] * eig_cols[...] + damping_term)).astype(bf16)
    back = lax.dot_general(scaled, basis[...], contract_last, preferred_element_type=f32)
    out[...] = jnp.dot(left[...], back.astype(bf16), preferred_element_type=f32)


def chain(rotated, basis, left, eig_rows, eig_cols):
    return pl.pallas_call(
        chain_kernel,
        in_specs=[pl.BlockSpec(memory_space=pltpu.VMEM)] * 5,
        out_specs=pl.BlockSpec(memory_space=pltpu.VMEM),
        out_shape=jax.ShapeDtypeStruct((left.shape[0], basis.shape[0]), f32),
        compiler_params=pltpu.CompilerParams(vmem_limit_bytes=32 << 20),
    )(rotated, basis, left, eig_rows, eig_cols)


def body(acts, grads, assign, bases_a, bases_g, eig_a, eig_g):
    n_proj = acts.shape[0]
    width = acts.shape[2]
    n_z, n_xl, n_core = (lax.axis_size(a) for a in DP)
    n_grp = lax.axis_size("xh") * lax.axis_size("y")
    n_dp = n_z * n_xl * n_core
    rows = width // n_dp
    tokens = acts.shape[1] * n_dp * n_grp
    z, xl, core = (lax.axis_index(a) for a in DP)

    def swap(x, axis):
        return lax.ppermute(x, axis, [(0, 1), (1, 0)])

    def in_order(index, mine, other):
        return jnp.where(index == 0, mine, other), jnp.where(index == 0, other, mine)

    mine = bases_g[0], bases_a[0]
    other, send = lax.optimization_barrier(
        ([swap(x, "xl") for x in mine], pick(assign, grads, acts))
    )
    mine = jnp.stack([jnp.stack(in_order(xl, *x)) for x in zip(mine, other)])
    pieces = [mine] * n_z
    up = down = mine
    for s in range(1, n_z // 2 + 1):
        pieces[s] = up = lax.ppermute(up, "z", [(i, (i + 1) % n_z) for i in range(n_z)])
        if s < n_z // 2:
            pieces[-s] = down = lax.ppermute(down, "z", [(i, (i - 1) % n_z) for i in range(n_z)])
    mine = order(lax.rem(z - jnp.arange(n_z, dtype=jnp.int32) + n_z, n_z), pieces)
    full_g, full_a = (x.reshape(width, width) for x in weave(core, mine, swap(mine, "core")))

    own = lax.all_to_all(send, GRP, 0, 0, tiled=True)
    own, full_g, full_a = lax.optimization_barrier((own, full_g, full_a))
    own_g = own[:, 0].reshape(-1, width)
    own_a = own[:, 1].reshape(-1, width)

    def dot_first(x, y):
        return lax.dot_general(x, y, contract_first, preferred_element_type=f32)

    def half_sum(parts, axis, index, dim):
        keep = lax.dynamic_index_in_dim(parts, index, dim, False)
        give = lax.dynamic_index_in_dim(parts, 1 - index, dim, False)
        return (keep.astype(f32) + swap(give.astype(bf16), axis).astype(f32)).astype(bf16)

    def core_sum(total):
        return half_sum(total.reshape(n_z, n_xl, n_core, rows, width), "core", core, 2)

    turned = jnp.dot(own_g, full_g, preferred_element_type=f32).astype(bf16)
    half = width // n_core
    give = lax.dynamic_slice_in_dim(turned, (1 - core) * half, half, 1)
    keep = lax.dynamic_slice_in_dim(turned, core * half, half, 1)
    give = swap(dot_first(give, own_a).astype(bf16), "core")
    kept = lax.optimization_barrier(dot_first(keep, own_a).astype(bf16))
    pair = (kept.astype(f32) + give.astype(f32)).astype(bf16)
    pair = pair.reshape(n_xl * n_z, rows, width)
    own_g, own_a, pair = lax.optimization_barrier((own_g, own_a, pair))
    half_g = core_sum(dot_first(own_g, own_g))
    half_a = core_sum(dot_first(own_a, own_a) / tokens)
    halves = jnp.concatenate([half_g, half_a], axis=2)
    keep = lax.optimization_barrier(lax.dynamic_index_in_dim(halves, xl, 1, False))
    give = swap(lax.dynamic_index_in_dim(halves, 1 - xl, 1, False), "xl")
    halves = (keep.astype(f32) + give.astype(f32)).astype(bf16)
    spread = spread_sum(lax.all_to_all(pair, ("xl", "z"), 0, 0, tiled=True), n_z)
    rotated = lax.all_to_all(spread, "z", 0, 0, tiled=True).reshape(n_z * rows, width)
    halves, _ = lax.optimization_barrier((halves, rotated))

    quarter = n_z * rows
    first = (core * n_xl + xl) * quarter
    eig_rows = lax.dynamic_slice_in_dim(eig_g[0], first, quarter, 0)
    family = n_xl * n_core * rows
    left = lax.dynamic_slice(full_g, (z * family, first), (family, quarter))
    left = left.reshape(n_xl, n_core, rows, quarter).swapaxes(0, 1).reshape(family, quarter)
    result = chain(rotated, full_a, left, eig_rows[:, None], eig_a)

    def fold(x, axis, index):
        halves = x.reshape(2, -1, width)
        keep = lax.dynamic_index_in_dim(halves, index, 0, False)
        give = lax.dynamic_index_in_dim(halves, 1 - index, 0, False)
        return keep + swap(give, axis)

    result = fold(result, "core", core)
    sums = jnp.sum(lax.all_to_all(halves, "z", 0, 0, tiled=True).astype(f32), axis=0)
    factor_g, factor_a = sums[:rows], sums[rows:]
    result = fold(result, "xl", xl).astype(bf16)
    n_y = lax.axis_size("y")
    pieces = [result] * n_grp
    hops = sorted(
        range(1, n_grp), key=lambda s: -(2 * (s // n_y) + min(s % n_y, n_y - s % n_y))
    )
    for s in hops:
        dx, dy = s // n_y, s % n_y
        moves = [
            (i, (i // n_y + dx) % (n_grp // n_y) * n_y + (i + dy) % n_y) for i in range(n_grp)
        ]
        pieces[s] = lax.ppermute(result, GRP, moves)
    dx = lax.rem(lax.axis_index("xh") - assign // n_y + n_grp // n_y, n_grp // n_y)
    dy = lax.rem(lax.axis_index("y") - lax.rem(assign, n_y) + n_y, n_y)
    index = (dx * n_y + dy)[:, None, None]
    precond = jnp.broadcast_to(pieces[0][None], (n_proj, rows, width))
    for s in range(1, n_grp):
        precond = jnp.where(index == s, pieces[s][None], precond)
    return (factor_a[None], factor_g[None], precond)


def solution(mesh):
    cut = Mesh(mesh.devices.reshape(8, 2, 2, 2, 4), DP + GRP)
    in_specs = (
        P(None, DP + GRP, None),
        P(None, DP + GRP, None),
        P(),
        P(GRP, DP, None),
        P(GRP, DP, None),
        P(GRP, None),
        P(GRP, None),
    )
    out_specs = (P(GRP, DP, None), P(GRP, DP, None), P(None, DP, None))
    return jax.shard_map(body, mesh=cut, in_specs=in_specs, out_specs=out_specs, check_vma=False)
```
